256 devices in a mesh: mp: 16 (over x_hi, z), dp: 16 (over x_lo, y, core).
Axes of the slice: x: 4 (x_hi: 2, x_lo: 2; x = x_hi * 2 + x_lo), y: 4, z: 8, core: 2. Of those that a mesh axis runs over, the one named last changes fastest.
Arguments:
- pre_act: bfloat16 [2048, 36864], P('dp', 'mp'), may hold values from -5 to 5
- cotangent: bfloat16 [2048, 10240], P('mp', 'dp'), may hold values from -6 to 6
- down_weight: bfloat16 [36864, 10240], P('mp', 'dp'), may hold values from -0.03125 to 0.03125
- first_moment: bfloat16 [36864, 10240], P('mp', 'dp'), may hold values from -8.125 to 8.125
- second_moment: bfloat16 [36864, 10240], P('mp', 'dp'), may hold values from 4.09375 to 204
Outputs:
- input_grad: bfloat16 [2048, 36864], P('dp', 'mp')
- step_update: bfloat16 [36864, 10240], P('mp', 'dp')
The draws below stay inside these ranges and needn't reach their ends.
All inputs are finite; a program needn't handle non-finite values.
Results may differ from the reference program's by a relative error of at most 0.023.
Values may be sent and summed in bfloat16 or wider, within the bound.
No kernel may reach another device: no remote copies, remote signals or barrier semaphores. Data moves between devices by JAX's collectives and lax.ppermute only.
A program may use at most 128 MiB of HBM per device.

```python
import math
import jax
import jax.numpy as jnp
from jax import lax

D = 10240
FF = 36864
STEP = 20
TOKENS = 2048
N_MP = 16
N_DP = 16


def levels(stream_key, shape, pieces, low, high):
    gain, own = 1.0, jax.random.fold_in(stream_key, 6)
    for dim, blocks in pieces:
        steps = jnp.exp(jax.random.uniform(jax.random.fold_in(own, dim), (blocks,), jnp.float32, low / len(pieces), high / len(pieces)))
        gain = gain * jnp.repeat(steps, shape[dim] // blocks).reshape([-1 if axis == dim else 1 for axis in range(len(shape))])
    return gain


def gaussian(rng, shape, spread, limit, split=(), kind=jnp.bfloat16):
    array = spread * jax.random.normal(rng, shape, jnp.float32)
    if split:
        array = array * levels(rng, shape, split, -0.22, 0.18)
    return jnp.clip(array, -limit, limit).astype(kind)


def setup_inputs(seed: int = 0) -> dict:
    streams_of = jax.random.split(jax.random.key(seed), 6)
    pre_act = gaussian(streams_of[0], (TOKENS, FF), 1.0, 5.0, ((0, 16), (1, 16)))
    cotangent = gaussian(streams_of[1], (TOKENS, D), 1.0, 6.0, ((0, 16), (1, 16)))
    down_weight = gaussian(streams_of[2], (FF, D), FF ** -0.5, 0.03125, ((0, 16), (1, 16)))
    first_moment = gaussian(streams_of[3], (FF, D), (0.03 * TOKENS ** 0.5), 8.125, ((0, 16), (1, 16)))
    second_moment = jnp.clip(jnp.exp(math.log(204.0) - 3.9086586 * jax.random.uniform(streams_of[4], (FF, D), jnp.float32) ** levels(streams_of[4], (FF, D), ((0, 16), (1, 16)), -0.2, 0.2)), 4.09375, 204.0).astype(jnp.bfloat16)
    return dict(pre_act=pre_act, cotangent=cotangent, down_weight=down_weight, first_moment=first_moment, second_moment=second_moment)


gelu_scale = 0.7978845608028654
gelu_cubic = 0.044715
beta_one = 0.9
beta_two = 0.95
epsilon = 1e-08

def gelu_parts(values):
    tangent = jnp.tanh(gelu_scale * (values + gelu_cubic * values * values * values))
    output = 0.5 * values * (1.0 + tangent)
    slopes = 0.5 * (1.0 + tangent) + 0.5 * values * (1.0 - tangent * tangent) * gelu_scale * (1.0 + 3.0 * gelu_cubic * values * values)
    return (output, slopes)

def adam_update(gradient, first_moment, second_moment):
    moment_one = beta_one * first_moment.astype(jnp.float32) + (1.0 - beta_one) * gradient
    moment_two = beta_two * second_moment.astype(jnp.float32) + (1.0 - beta_two) * gradient * gradient
    corrected = moment_one / (1.0 - beta_one ** STEP)
    scaled = jnp.sqrt(moment_two / (1.0 - beta_two ** STEP))
    return (corrected / (scaled + epsilon)).astype(jnp.bfloat16)

def reference(pre_act, cotangent, down_weight, first_moment, second_moment):
    output, slopes = gelu_parts(pre_act.astype(jnp.float32))
    hidden = output.astype(jnp.bfloat16)
    columns = D // N_DP

    def add_block(block_index, summed):
        offset = (block_index * columns).astype(jnp.int32)
        cot_block = lax.dynamic_slice_in_dim(cotangent, offset, columns, 1)
        weight_block = lax.dynamic_slice_in_dim(down_weight, offset, columns, 1)
        partial_sum = lax.dot_general(cot_block, weight_block, (((1,), (1,)), ((), ())), preferred_element_type=jnp.float32)
        rounded = lax.optimization_barrier(partial_sum.astype(jnp.bfloat16))
        return summed + rounded.astype(jnp.float32)
    hidden_grad = lax.fori_loop(0, N_DP, add_block, jnp.zeros((TOKENS, FF), jnp.float32))
    input_grad = (hidden_grad * slopes).astype(jnp.bfloat16)
    unit_rows = FF // N_MP

    def block_update(block_index):
        offset = (block_index * unit_rows).astype(jnp.int32)
        hidden_block = lax.dynamic_slice_in_dim(hidden, offset, unit_rows, 1)
        gradient = lax.dot_general(hidden_block, cotangent, (((0,), (0,)), ((), ())), preferred_element_type=jnp.float32)
        moment_block = lax.dynamic_slice_in_dim(first_moment, offset, unit_rows, 0)
        second_block = lax.dynamic_slice_in_dim(second_moment, offset, unit_rows, 0)
        return adam_update(gradient, moment_block, second_block)
    stacked = lax.map(block_update, jnp.arange(N_MP, dtype=jnp.int32))
    return (input_grad, stacked.reshape(FF, D))
```

```python
import jax
import jax.numpy as jnp
from jax import lax
from jax.sharding import PartitionSpec as P

STEP = 20

gelu_scale = 0.7978845608028654
gelu_cubic = 0.044715
beta_one = 0.9
beta_two = 0.95
epsilon = 1e-08

f32 = jnp.float32
bf16 = jnp.bfloat16


def gelu_parts(values):
    tangent = jnp.tanh(gelu_scale * (values + gelu_cubic * values * values * values))
    output = 0.5 * values * (1.0 + tangent)
    slopes = 0.5 * (1.0 + tangent) + 0.5 * values * (1.0 - tangent * tangent) * gelu_scale * (
        1.0 + 3.0 * gelu_cubic * values * values
    )
    return (output, slopes)


def adam_update(gradient, first_moment, second_moment):
    moment_one = beta_one * first_moment.astype(f32) + (1.0 - beta_one) * gradient
    moment_two = beta_two * second_moment.astype(f32) + (1.0 - beta_two) * gradient * gradient
    corrected = moment_one / (1.0 - beta_one**STEP)
    scaled = jnp.sqrt(moment_two / (1.0 - beta_two**STEP))
    return (corrected / (scaled + epsilon)).astype(bf16)


def move_dp(x, dx, dy, dc):
    pairs = [
        (i, ((i // 8 + dx) % 2) * 8 + ((i // 2 + dy) % 4) * 2 + (i + dc) % 2) for i in range(16)
    ]
    return lax.ppermute(x, "dp", pairs)


def move_mp(x, dx, dz):
    pairs = [(i, ((i // 8 + dx) % 2) * 8 + (i + dz) % 8) for i in range(16)]
    return lax.ppermute(x, "mp", pairs)


def third(x, i):
    size = x.shape[1] // 3
    return x[:, i * size : (i + 1) * size]


def gather_mp(block):
    both = jnp.stack([block, move_mp(block, 1, 0)])
    up, down = [both], [both]
    for _ in range(3):
        up.append(move_mp(up[-1], 0, 1))
        down.append(move_mp(down[-1], 0, -1))
    far = jnp.concatenate([move_mp(up[-1][:1], 0, 1), move_mp(down[-1][1:], 0, -1)])
    parts = [both, down[1], down[2], down[3], far, up[3], up[2], up[1]]
    return jnp.stack(parts, axis=1).reshape(16, *block.shape)


ORDER = ((1, 2), (1, 1), (1, 3), (0, 2), (0, 1), (0, 3), (1, 0), (0, 0))


def gather_dp(block):
    y_prev = move_dp(block, 0, 1, 0)
    y_next = move_dp(block, 0, -1, 0)
    x_other = move_dp(block, 1, 0, 0)
    xy_next = move_dp(y_next, 1, 0, 0)
    xy_prev = move_dp(x_other, 0, 1, 0)
    y_far = move_dp(y_next, 0, -1, 0)
    xy_far = jnp.concatenate(
        [
            move_dp(third(xy_next, 0), 0, -1, 0),
            move_dp(third(xy_prev, 1), 0, 1, 0),
            move_dp(third(y_far, 2), 1, 0, 0),
        ],
        axis=1,
    )
    return jnp.concatenate([xy_far, xy_next, xy_prev, y_far, y_next, y_prev, x_other, block], axis=0)


def add(*terms):
    return sum(t.astype(f32) for t in terms).astype(bf16)


def add_third(x, i, got):
    return jnp.concatenate(
        [add(third(x, k), got) if k == i else third(x, k) for k in range(3)], axis=1
    )


def shards(pre_act, cotangent, down_weight, first_moment, second_moment):
    rows, units = pre_act.shape
    core = lax.axis_index("dp") % 2
    y = (lax.axis_index("dp") // 2) % 4
    x_lo = lax.axis_index("dp") // 8
    x_hi = lax.axis_index("mp") // 8
    z = lax.axis_index("mp") % 8
    contract_rows = (((0,), (0,)), ((), ()))
    contract_cols = (((1,), (1,)), ((), ()))

    hidden = gelu_parts(pre_act.astype(f32))[0].astype(bf16)
    weight = jnp.concatenate([down_weight, move_dp(down_weight, 0, 0, 1)], axis=1)

    cot = gather_mp(cotangent)

    def place(dx, dy, parity):
        z_of = ((y + dy) % 4) * 2 + parity
        return ((x_lo + dx - x_hi) % 2) * 8 + (z_of - z) % 8

    def pick(parity):
        return jnp.concatenate(
            [lax.dynamic_index_in_dim(cot, place(dx, dy, parity), 0, False) for dx, dy in ORDER],
            axis=0,
        )

    cot_own = pick(core)
    cot_give = pick(1 - core)
    cot_got = move_dp(cot_give, 0, 0, 1)
    cot_wide = jnp.concatenate([cot_own, cot_got], axis=1)

    def partial(lo, hi):
        return lax.optimization_barrier(
            lax.dot_general(
                cot_wide[lo * rows : hi * rows], weight, contract_cols, preferred_element_type=f32
            ).astype(bf16)
        )

    hid = gather_dp(hidden)
    hid, cot_wide = lax.optimization_barrier((hid, cot_wide))

    xy_far = partial(0, 1)
    got0 = move_dp(third(xy_far, 0), 0, 1, 0)
    got1 = move_dp(third(xy_far, 1), 0, -1, 0)
    got2 = move_dp(third(xy_far, 2), 1, 0, 0)
    mid = partial(1, 4)
    near = partial(4, 8)
    xy_next, xy_prev, y_far = mid[:rows], mid[rows : 2 * rows], mid[2 * rows :]
    y_next, y_prev, x_other, mine = (near[k * rows : (k + 1) * rows] for k in range(4))
    got0, got1, got2 = lax.optimization_barrier((got0, got1, got2))
    got_x = move_dp(add_third(xy_next, 0, got0), 1, 0, 0)
    got_m = move_dp(add_third(xy_prev, 1, got1), 0, -1, 0)
    got_y = move_dp(add_third(y_far, 2, got2), 0, 1, 0)
    got_x, got_m, got_y = lax.optimization_barrier((got_x, got_m, got_y))
    end_prev = move_dp(y_prev, 0, -1, 0)
    end_next = move_dp(add(y_next, got_x, got_y), 0, 1, 0)
    end_x = move_dp(add(x_other, got_m), 1, 0, 0)

    hid_other = move_dp(hid, 0, 0, 1)
    gradient = lax.dot_general(hid, cot_own, contract_rows, preferred_element_type=f32)
    gradient += lax.dot_general(hid_other, cot_give, contract_rows, preferred_element_type=f32)
    step_update = adam_update(gradient, first_moment, second_moment)

    hidden_grad = sum(t.astype(f32) for t in (mine, end_prev, end_next, end_x))
    slopes = gelu_parts(pre_act.astype(f32))[1]
    return ((hidden_grad * slopes).astype(bf16), step_update)


def solution(mesh):
    placed = (P("dp", "mp"), P("mp", "dp"), P("mp", "dp"), P("mp", "dp"), P("mp", "dp"))
    return jax.shard_map(
        shards,
        mesh=mesh,
        in_specs=placed,
        out_specs=(P("dp", "mp"), P("mp", "dp")),
        check_vma=False,
    )
```

```python
import functools

import jax
import jax.numpy as jnp
from jax import lax
from jax.experimental import pallas as pl
from jax.experimental.pallas import tpu as pltpu
from jax.sharding import PartitionSpec as P

STEP = 20

gelu_scale = 0.7978845608028654
gelu_cubic = 0.044715
beta_one = 0.9
beta_two = 0.95
epsilon = 1e-08

f32 = jnp.float32
bf16 = jnp.bfloat16
barrier = lax.optimization_barrier
VMEM = 40 << 20


def gelu_parts(values):
    tangent = jnp.tanh(gelu_scale * (values + gelu_cubic * values * values * values))
    output = 0.5 * values * (1.0 + tangent)
    slopes = 0.5 * (1.0 + tangent) + 0.5 * values * (1.0 - tangent * tangent) * gelu_scale * (
        1.0 + 3.0 * gelu_cubic * values * values
    )
    return (output, slopes)


def adam_update(gradient, first_moment, second_moment):
    scale_one = 1.0 / (1.0 - beta_one**STEP)
    scale_two = 1.0 / (1.0 - beta_two**STEP)
    corrected = (beta_one * scale_one) * first_moment.astype(f32)
    corrected += ((1.0 - beta_one) * scale_one) * gradient
    scaled = (beta_two * scale_two) * second_moment.astype(f32)
    scaled += ((1.0 - beta_two) * scale_two) * (gradient * gradient)
    return (corrected / (jnp.sqrt(scaled) + epsilon)).astype(bf16)


def move_dp(x, dx, dy, dc):
    pairs = [
        (i, ((i // 8 + dx) % 2) * 8 + ((i // 2 + dy) % 4) * 2 + (i + dc) % 2) for i in range(16)
    ]
    return lax.ppermute(x, "dp", pairs)


def move_mp(x, dx, dz):
    pairs = [(i, ((i // 8 + dx) % 2) * 8 + (i + dz) % 8) for i in range(16)]
    return lax.ppermute(x, "mp", pairs)


ORDER = ((1, 2), (1, 1), (1, 3), (0, 2), (0, 1), (0, 3), (1, 0), (0, 0))


def turn_kernel(pre_act, hidden):
    hidden[...] = gelu_parts(pre_act[...].astype(f32))[0].T.astype(bf16)


def slope_kernel(pre_act, slopes):
    slopes[...] = gelu_parts(pre_act[...].astype(f32))[1]


def local(kernel, pre_act, turn, dtype, cost, tile=768):
    rows, units = pre_act.shape
    across = pl.BlockSpec((rows, tile), lambda j: (0, j))
    along = pl.BlockSpec((tile, rows), lambda j: (j, 0))
    return pl.pallas_call(
        kernel,
        grid=(units // tile,),
        in_specs=[across],
        out_specs=along if turn else across,
        out_shape=jax.ShapeDtypeStruct((units, rows) if turn else (rows, units), dtype),
        cost_estimate=pl.CostEstimate(
            flops=20 * rows * units, bytes_accessed=cost, transcendentals=rows * units
        ),
    )(pre_act)


def gradient_kernel(thirds, per, *refs):
    pieces, (cot, own, other, first) = refs[thirds:-4], refs[-4:]
    width = first.shape[1]
    for n in range(thirds):

        @pl.when(pl.program_id(0) // per == n)
        def _(n=n):
            first[...] = refs[n][...]

    hidden = jnp.concatenate([first[...], *(ref[...] for ref in pieces)], axis=1)
    half = own.shape[1]
    gradient = jnp.dot(hidden, cot[...], preferred_element_type=f32)
    own[...] = gradient[:, :half]
    other[...] = gradient[:, half:].astype(bf16)


def gradients(thirds, pieces, cot, tile):
    units, rows = pieces[0].shape
    tokens, features = cot.shape
    per = thirds[0].shape[0] // tile
    specs = [
        pl.BlockSpec((tile, rows), lambda j, n=n: (jnp.clip(j - n * per, 0, per - 1), 0))
        for n in range(len(thirds))
    ]
    specs += [pl.BlockSpec((tile, rows), lambda j: (j, 0))] * len(pieces)
    specs += [pl.BlockSpec((tokens, features), lambda j: (0, 0))]
    out = pl.BlockSpec((tile, features // 2), lambda j: (j, 0))
    return pl.pallas_call(
        functools.partial(gradient_kernel, len(thirds), per),
        grid=(units // tile,),
        in_specs=specs,
        out_specs=[out, out],
        out_shape=[
            jax.ShapeDtypeStruct((units, features // 2), f32),
            jax.ShapeDtypeStruct((units, features // 2), bf16),
        ],
        scratch_shapes=[pltpu.VMEM((tile, rows), bf16)],
        compiler_params=pltpu.CompilerParams(vmem_limit_bytes=VMEM),
        cost_estimate=pl.CostEstimate(
            flops=2 * tokens * units * features, bytes_accessed=18 << 20, transcendentals=0
        ),
    )(*thirds, *pieces, cot)


def adam_kernel(own, got, first, second, out):
    out[...] = adam_update(own[...] + got[...].astype(f32), first[...], second[...])


def adam(own, got, first_moment, second_moment, tile):
    units, features = own.shape
    block = pl.BlockSpec((tile, features), lambda j: (j, 0))
    return pl.pallas_call(
        adam_kernel,
        grid=(units // tile,),
        in_specs=[block] * 4,
        out_specs=block,
        out_shape=jax.ShapeDtypeStruct((units, features), bf16),
        compiler_params=pltpu.CompilerParams(vmem_limit_bytes=24 << 20),
        cost_estimate=pl.CostEstimate(
            flops=0, bytes_accessed=12 * units * features, transcendentals=0
        ),
    )(own, got, first_moment, second_moment)


def places(dp, mp):
    block = jnp.arange(16, dtype=jnp.int32)
    z = (mp + block) % 8
    code = ((mp // 8 + block // 8 + dp // 8) % 2) * 4 + (z // 2 - dp // 2) % 4
    slot = sum(jnp.where(code == dx * 4 + dy, i, 0) for i, (dx, dy) in enumerate(ORDER))
    return (slot + 8 * ((z + dp) % 2)).astype(jnp.int32)


def collect_kernel(plan, where, *refs):
    pieces, (own, give) = refs[:-2], refs[-2:]
    depth = pieces[0].shape[1]
    for piece, part, block in plan:
        row = pl.multiple_of(where[block] % 8 * depth, depth)

        @pl.when(where[block] < 8)
        def _():
            own[pl.ds(row, depth)] = pieces[piece][part]

        @pl.when(where[block] >= 8)
        def _():
            give[pl.ds(row, depth)] = pieces[piece][part]


def collect(where, pieces, plan):
    depth, width = pieces[0].shape[1:]
    whole = lambda shape: pl.BlockSpec(shape, lambda j, w: (0,) * len(shape))
    shape = (8 * depth, width)
    return pl.pallas_call(
        functools.partial(collect_kernel, plan),
        out_shape=[jax.ShapeDtypeStruct(shape, bf16)] * 2,
        grid_spec=pltpu.PrefetchScalarGridSpec(
            num_scalar_prefetch=1,
            grid=(1,),
            in_specs=[whole(p.shape) for p in pieces],
            out_specs=[whole(shape)] * 2,
        ),
        compiler_params=pltpu.CompilerParams(vmem_limit_bytes=16 << 20),
        cost_estimate=pl.CostEstimate(
            flops=0, bytes_accessed=60 * depth * width, transcendentals=0
        ),
    )(where, *pieces)


def swap(x):
    return move_dp(x, 0, 0, 1)


def add(*terms):
    return sum(t.astype(f32) for t in terms).astype(bf16)


def add_third(x, i, got):
    size = got.shape[1]
    return add(x, jnp.pad(got, ((0, 0), (i * size, (2 - i) * size))))


def shards(pre_act, cotangent, down_weight, first_moment, second_moment):
    rows, units = pre_act.shape
    features = cotangent.shape[1]
    dp = lax.axis_index("dp")
    mp = lax.axis_index("mp")
    contract_cols = (((1,), (1,)), ((), ()))

    partner = move_mp(cotangent, 1, 0)
    weight = move_dp(down_weight, 0, 0, 1)
    hidden = local(turn_kernel, pre_act, True, bf16, 32 << 20)
    where = places(dp, mp)
    partner, where, _ = barrier((partner, where, hidden))

    both = jnp.stack([cotangent, partner])
    up, down = [both], [both]
    weight = jnp.concatenate([down_weight, weight], axis=1)
    slopes = local(slope_kernel, pre_act, False, f32, 16 << 20)
    for n in range(3):
        up.append(move_mp(up[-1], 0, 1))
        down.append(move_mp(down[-1], 0, -1))
        if n == 0:
            up[1], down[1], weight, slopes = barrier((up[1], down[1], weight, slopes))
    x_other = move_dp(hidden, 1, 0, 0)
    y_prev = move_dp(hidden, 0, 1, 0)
    y_next = move_dp(hidden, 0, -1, 0)
    x_other, y_prev = barrier((x_other, y_prev))
    xy_next = move_dp(y_next, 1, 0, 0)
    xy_prev = move_dp(x_other, 0, 1, 0)
    y_far = move_dp(y_next, 0, -1, 0)
    up[3], down[3], xy_next, xy_prev, y_far = barrier(
        (up[3], down[3], xy_next, xy_prev, y_far)
    )
    size = units // 3
    cut = lambda x, i: x[i * size : (i + 1) * size]
    xy_far = [
        move_dp(cut(xy_next, 0), 0, -1, 0),
        move_dp(cut(xy_prev, 1), 0, 1, 0),
        move_dp(cut(y_far, 2), 1, 0, 0),
    ]
    pieces = [both, *down[1:], *up[1:], move_mp(up[3][:1], 0, 1), move_mp(down[3][1:], 0, -1)]
    plan = [(n, f, 8 * f + (n if n < 4 else 11 - n)) for n in range(7) for f in range(2)]
    plan += [(7, 0, 4), (8, 0, 12)]
    cot_own, cot_give = collect(where, barrier(pieces), plan)
    cot_wide = jnp.concatenate([cot_own, swap(cot_give)], axis=1)

    def partial(lo, hi):
        return barrier(
            lax.dot_general(
                cot_wide[lo * rows : hi * rows], weight, contract_cols, preferred_element_type=f32
            ).astype(bf16)
        )

    split = lambda x: [x[k * rows : (k + 1) * rows] for k in range(4)]
    third = lambda x, i: x[:, i * size : (i + 1) * size]
    p_far, p_xy_next, p_xy_prev, p_y_far = split(partial(0, 4))
    got0 = move_dp(third(p_far, 0), 0, 1, 0)
    got1 = move_dp(third(p_far, 1), 0, -1, 0)
    got2 = move_dp(third(p_far, 2), 1, 0, 0)
    near = partial(4, 8)
    got0, got1, got2, near, cot_wide, xy_far = barrier(
        (got0, got1, got2, near, cot_wide, xy_far)
    )
    p_next, p_prev, p_x, p_mine = split(near)
    got_x = move_dp(add_third(p_xy_next, 0, got0), 1, 0, 0)
    got_m = move_dp(add_third(p_xy_prev, 1, got1), 0, -1, 0)
    got_y = move_dp(add_third(p_y_far, 2, got2), 0, 1, 0)
    sent = [xy_next, xy_prev, y_far, y_next, y_prev, x_other, hidden]
    grad_own, grad_give = gradients(xy_far, sent, cot_wide, units // 3)
    got_x, got_m, got_y, grad_own, grad_give, p_prev = barrier(
        (got_x, got_m, got_y, grad_own, grad_give, p_prev)
    )
    p_next, p_x, grad_give = barrier((add(p_next, got_x, got_y), add(p_x, got_m), grad_give))
    end_next = move_dp(p_next, 0, 1, 0)
    end_x = move_dp(p_x, 1, 0, 0)
    end_prev = move_dp(p_prev, 0, -1, 0)
    step_update = adam(grad_own, swap(grad_give), first_moment, second_moment, units // 6)
    end_prev, end_next, end_x, step_update = barrier((end_prev, end_next, end_x, step_update))

    hidden_grad = sum(t.astype(f32) for t in (p_mine, end_prev, end_next, end_x))
    return ((hidden_grad * slopes).astype(bf16), step_update)


def solution(mesh):
    placed = (P("dp", "mp"), P("mp", "dp"), P("mp", "dp"), P("mp", "dp"), P("mp", "dp"))
    return jax.shard_map(
        shards,
        mesh=mesh,
        in_specs=placed,
        out_specs=(P("dp", "mp"), P("mp", "dp")),
        check_vma=False,
    )
```

```python
import functools

import jax
import jax.numpy as jnp
from jax import lax
from jax.experimental import pallas as pl
from jax.experimental.pallas import tpu as pltpu
from jax.sharding import PartitionSpec as P

STEP = 20

gelu_scale = 0.7978845608028654
gelu_cubic = 0.044715
beta_one = 0.9
beta_two = 0.95
epsilon = 1e-08

f32 = jnp.float32
bf16 = jnp.bfloat16
barrier = lax.optimization_barrier
VMEM = 40 << 20


def gelu_parts(values):
    tangent = jnp.tanh(gelu_scale * (values + gelu_cubic * values * values * values))
    output = 0.5 * values * (1.0 + tangent)
    slopes = 0.5 * (1.0 + tangent) + 0.5 * values * (1.0 - tangent * tangent) * gelu_scale * (
        1.0 + 3.0 * gelu_cubic * values * values
    )
    return (output, slopes)


def adam_update(gradient, first_moment, second_moment):
    scale_one = 1.0 / (1.0 - beta_one**STEP)
    scale_two = 1.0 / (1.0 - beta_two**STEP)
    corrected = (beta_one * scale_one) * first_moment.astype(f32)
    corrected += ((1.0 - beta_one) * scale_one) * gradient
    scaled = (beta_two * scale_two) * second_moment.astype(f32)
    scaled += ((1.0 - beta_two) * scale_two) * (gradient * gradient)
    return (corrected / (jnp.sqrt(scaled) + epsilon)).astype(bf16)


def move_dp(x, dx, dy, dc):
    pairs = [
        (i, ((i // 8 + dx) % 2) * 8 + ((i // 2 + dy) % 4) * 2 + (i + dc) % 2) for i in range(16)
    ]
    return lax.ppermute(x, "dp", pairs)


def move_mp(x, dx, dz):
    pairs = [(i, ((i // 8 + dx) % 2) * 8 + (i + dz) % 8) for i in range(16)]
    return lax.ppermute(x, "mp", pairs)


ORDER = ((1, 2), (1, 1), (1, 3), (0, 2), (0, 1), (0, 3), (1, 0), (0, 0))


def turn_kernel(pre_act, hidden):
    hidden[...] = gelu_parts(pre_act[...].astype(f32))[0].astype(bf16).T


def slope_kernel(pre_act, slopes):
    slopes[...] = gelu_parts(pre_act[...].astype(f32))[1]


def local(kernel, pre_act, turn, dtype, cost, tile=1152):
    rows, units = pre_act.shape
    across = pl.BlockSpec((rows, tile), lambda j: (0, j))
    along = pl.BlockSpec((tile, rows), lambda j: (j, 0))
    return pl.pallas_call(
        kernel,
        grid=(units // tile,),
        in_specs=[across],
        out_specs=along if turn else across,
        out_shape=jax.ShapeDtypeStruct((units, rows) if turn else (rows, units), dtype),
        cost_estimate=pl.CostEstimate(
            flops=20 * rows * units, bytes_accessed=cost, transcendentals=rows * units
        ),
    )(pre_act)


def gradient_kernel(thirds, per, *refs):
    pieces, (cot, own, other, first) = refs[thirds:-4], refs[-4:]
    width = first.shape[1]
    for n in range(thirds):

        @pl.when(pl.program_id(0) // per == n)
        def _(n=n):
            first[...] = refs[n][...]

    hidden = jnp.concatenate([first[...], *(ref[...] for ref in pieces)], axis=1)
    half = own.shape[1]
    gradient = jnp.dot(hidden, cot[...], preferred_element_type=f32)
    own[...] = gradient[:, :half]
    other[...] = gradient[:, half:].astype(bf16)


def gradients(thirds, pieces, cot, tile):
    units, rows = pieces[0].shape
    tokens, features = cot.shape
    per = thirds[0].shape[0] // tile
    specs = [
        pl.BlockSpec((tile, rows), lambda j, n=n: (jnp.clip(j - n * per, 0, per - 1), 0))
        for n in range(len(thirds))
    ]
    specs += [pl.BlockSpec((tile, rows), lambda j: (j, 0))] * len(pieces)
    specs += [pl.BlockSpec((tokens, features), lambda j: (0, 0))]
    out = pl.BlockSpec((tile, features // 2), lambda j: (j, 0))
    return pl.pallas_call(
        functools.partial(gradient_kernel, len(thirds), per),
        grid=(units // tile,),
        in_specs=specs,
        out_specs=[out, out],
        out_shape=[
            jax.ShapeDtypeStruct((units, features // 2), f32),
            jax.ShapeDtypeStruct((units, features // 2), bf16),
        ],
        scratch_shapes=[pltpu.VMEM((tile, rows), bf16)],
        compiler_params=pltpu.CompilerParams(vmem_limit_bytes=VMEM),
        cost_estimate=pl.CostEstimate(
            flops=2 * tokens * units * features, bytes_accessed=18 << 20, transcendentals=0
        ),
    )(*thirds, *pieces, cot)


def adam_kernel(own, got, first, second, out):
    out[...] = adam_update(own[...] + got[...].astype(f32), first[...], second[...])


def adam(own, got, first_moment, second_moment, tile):
    units, features = own.shape
    block = pl.BlockSpec((tile, features), lambda j: (j, 0))
    return pl.pallas_call(
        adam_kernel,
        grid=(units // tile,),
        in_specs=[block] * 4,
        out_specs=block,
        out_shape=jax.ShapeDtypeStruct((units, features), bf16),
        compiler_params=pltpu.CompilerParams(vmem_limit_bytes=24 << 20),
        cost_estimate=pl.CostEstimate(
            flops=0, bytes_accessed=12 * units * features, transcendentals=0
        ),
    )(own, got, first_moment, second_moment)


def places(dp, mp):
    block = jnp.arange(16, dtype=jnp.int32)
    z = (mp + block) % 8
    code = ((mp // 8 + block // 8 + dp // 8) % 2) * 4 + (z // 2 - dp // 2) % 4
    slot = sum(jnp.where(code == dx * 4 + dy, i, 0) for i, (dx, dy) in enumerate(ORDER))
    return (slot + 8 * ((z + dp) % 2)).astype(jnp.int32)


def collect_kernel(plan, where, *refs):
    pieces, (own, give) = refs[:-2], refs[-2:]
    depth = pieces[0].shape[1]
    for piece, part, block in plan:
        row = pl.multiple_of(where[block] % 8 * depth, depth)

        @pl.when(where[block] < 8)
        def _():
            own[pl.ds(row, depth)] = pieces[piece][part]

        @pl.when(where[block] >= 8)
        def _():
            give[pl.ds(row, depth)] = pieces[piece][part]


def collect(where, pieces, plan):
    depth, width = pieces[0].shape[1:]
    whole = lambda shape: pl.BlockSpec(shape, lambda j, w: (0,) * len(shape))
    shape = (8 * depth, width)
    return pl.pallas_call(
        functools.partial(collect_kernel, plan),
        out_shape=[jax.ShapeDtypeStruct(shape, bf16)] * 2,
        grid_spec=pltpu.PrefetchScalarGridSpec(
            num_scalar_prefetch=1,
            grid=(1,),
            in_specs=[whole(p.shape) for p in pieces],
            out_specs=[whole(shape)] * 2,
        ),
        compiler_params=pltpu.CompilerParams(vmem_limit_bytes=16 << 20),
        cost_estimate=pl.CostEstimate(
            flops=0, bytes_accessed=60 * depth * width, transcendentals=0
        ),
    )(where, *pieces)


def swap(x):
    return move_dp(x, 0, 0, 1)


def add(*terms):
    return sum(t.astype(f32) for t in terms).astype(bf16)


def add_third(x, i, got):
    size = got.shape[1]
    return add(x, jnp.pad(got, ((0, 0), (i * size, (2 - i) * size))))


def shards(pre_act, cotangent, down_weight, first_moment, second_moment):
    rows, units = pre_act.shape
    features = cotangent.shape[1]
    dp = lax.axis_index("dp")
    mp = lax.axis_index("mp")
    contract_cols = (((1,), (1,)), ((), ()))

    partner = move_mp(cotangent, 1, 0)
    weight = move_dp(down_weight, 0, 0, 1)
    hidden = local(turn_kernel, pre_act, True, bf16, 32 << 20)
    where = places(dp, mp)
    partner, where, _ = barrier((partner, where, hidden))

    both = jnp.stack([cotangent, partner])
    up, down = [both], [both]
    weight = jnp.concatenate([down_weight, weight], axis=1)
    for n in range(3):
        up.append(move_mp(up[-1], 0, 1))
        down.append(move_mp(down[-1], 0, -1))
        if n == 0:
            up[1], down[1], weight = barrier((up[1], down[1], weight))
    x_other = move_dp(hidden, 1, 0, 0)
    y_prev = move_dp(hidden, 0, 1, 0)
    y_next = move_dp(hidden, 0, -1, 0)
    x_other, y_prev = barrier((x_other, y_prev))
    y_far = move_dp(y_next, 0, -1, 0)
    xy_prev = move_dp(x_other, 0, 1, 0)
    xy_next = move_dp(y_next, 1, 0, 0)
    up[3], down[3], y_far, xy_prev, xy_next = barrier(
        (up[3], down[3], y_far, xy_prev, xy_next)
    )
    size = units // 3
    cut = lambda x, i: x[i * size : (i + 1) * size]
    xy_far = [
        move_dp(cut(xy_next, 0), 0, -1, 0),
        move_dp(cut(xy_prev, 1), 0, 1, 0),
        move_dp(cut(y_far, 2), 1, 0, 0),
    ]
    pieces = [both, *down[1:], *up[1:], move_mp(up[3][:1], 0, 1), move_mp(down[3][1:], 0, -1)]
    plan = [(n, f, 8 * f + (n if n < 4 else 11 - n)) for n in range(7) for f in range(2)]
    plan += [(7, 0, 4), (8, 0, 12)]
    cot_own, cot_give = collect(where, barrier(pieces), plan)
    cot_wide = jnp.concatenate([cot_own, swap(cot_give)], axis=1)

    def partial(lo, hi):
        return barrier(
            lax.dot_general(
                cot_wide[lo * rows : hi * rows], weight, contract_cols, preferred_element_type=f32
            ).astype(bf16)
        )

    split = lambda x: [x[k * rows : (k + 1) * rows] for k in range(7)]
    third = lambda x, i: x[:, i * size : (i + 1) * size]
    p_far = partial(0, 1)
    got0 = move_dp(third(p_far, 0), 0, 1, 0)
    got1 = move_dp(third(p_far, 1), 0, -1, 0)
    got2 = move_dp(third(p_far, 2), 1, 0, 0)
    rest = partial(1, 8)
    got0, got1, got2, rest, cot_wide, xy_far = barrier(
        (got0, got1, got2, rest, cot_wide, xy_far)
    )
    p_xy_next, p_xy_prev, p_y_far, p_next, p_prev, p_x, p_mine = split(rest)
    got_x = move_dp(add_third(p_xy_next, 0, got0), 1, 0, 0)
    got_m = move_dp(add_third(p_xy_prev, 1, got1), 0, -1, 0)
    got_y = move_dp(add_third(p_y_far, 2, got2), 0, 1, 0)
    sent = [xy_next, xy_prev, y_far, y_next, y_prev, x_other, hidden]
    grad_own, grad_give = gradients(xy_far, sent, cot_wide, units // 3)
    got_x, got_m, got_y, grad_own, grad_give, p_prev = barrier(
        (got_x, got_m, got_y, grad_own, grad_give, p_prev)
    )
    p_next, p_x, grad_give = barrier((add(p_next, got_x, got_y), add(p_x, got_m), grad_give))
    end_next = move_dp(p_next, 0, 1, 0)
    end_x = move_dp(p_x, 1, 0, 0)
    end_prev = move_dp(p_prev, 0, -1, 0)
    step_update = adam(grad_own, swap(grad_give), first_moment, second_moment, units // 6)
    step_update, pre_act = barrier((step_update, pre_act))
    slopes = local(slope_kernel, pre_act, False, f32, 1)
    end_prev, end_next, end_x, slopes = barrier((end_prev, end_next, end_x, slopes))

    hidden_grad = sum(t.astype(f32) for t in (p_mine, end_prev, end_next, end_x))
    return ((hidden_grad * slopes).astype(bf16), step_update)


def solution(mesh):
    placed = (P("dp", "mp"), P("mp", "dp"), P("mp", "dp"), P("mp", "dp"), P("mp", "dp"))
    return jax.shard_map(
        shards,
        mesh=mesh,
        in_specs=placed,
        out_specs=(P("dp", "mp"), P("mp", "dp")),
        check_vma=False,
    )
```

```python
import functools

import jax
import jax.numpy as jnp
from jax import lax
from jax.experimental import pallas as pl
from jax.experimental.pallas import tpu as pltpu
from jax.sharding import PartitionSpec as P

STEP = 20

gelu_scale = 0.7978845608028654
gelu_cubic = 0.044715
beta_one = 0.9
beta_two = 0.95
epsilon = 1e-08

f32 = jnp.float32
bf16 = jnp.bfloat16
barrier = lax.optimization_barrier
VMEM = 40 << 20


def gelu_parts(values):
    tangent = jnp.tanh(gelu_scale * (values + gelu_cubic * values * values * values))
    output = 0.5 * values * (1.0 + tangent)
    slopes = 0.5 * (1.0 + tangent) + 0.5 * values * (1.0 - tangent * tangent) * gelu_scale * (
        1.0 + 3.0 * gelu_cubic * values * values
    )
    return (output, slopes)


def adam_update(gradient, first_moment, second_moment):
    scale_one = 1.0 / (1.0 - beta_one**STEP)
    scale_two = 1.0 / (1.0 - beta_two**STEP)
    corrected = (beta_one * scale_one) * first_moment.astype(f32)
    corrected += ((1.0 - beta_one) * scale_one) * gradient
    scaled = (beta_two * scale_two) * second_moment.astype(f32)
    scaled += ((1.0 - beta_two) * scale_two) * (gradient * gradient)
    return (corrected / (jnp.sqrt(scaled) + epsilon)).astype(bf16)


def move_dp(x, dx, dy, dc):
    pairs = [
        (i, ((i // 8 + dx) % 2) * 8 + ((i // 2 + dy) % 4) * 2 + (i + dc) % 2) for i in range(16)
    ]
    return lax.ppermute(x, "dp", pairs)


def move_mp(x, dx, dz):
    pairs = [(i, ((i // 8 + dx) % 2) * 8 + (i + dz) % 8) for i in range(16)]
    return lax.ppermute(x, "mp", pairs)


ORDER = ((1, 2), (1, 1), (1, 3), (0, 2), (0, 1), (0, 3), (1, 0), (0, 0))


def turn_kernel(pre_act, hidden):
    hidden[...] = gelu_parts(pre_act[...].astype(f32))[0].astype(bf16).T


def slope_kernel(pre_act, slopes):
    slopes[...] = gelu_parts(pre_act[...].astype(f32))[1]


def local(kernel, pre_act, turn, dtype, cost, tile=1152):
    rows, units = pre_act.shape
    across = pl.BlockSpec((rows, tile), lambda j: (0, j))
    along = pl.BlockSpec((tile, rows), lambda j: (j, 0))
    return pl.pallas_call(
        kernel,
        grid=(units // tile,),
        in_specs=[across],
        out_specs=along if turn else across,
        out_shape=jax.ShapeDtypeStruct((units, rows) if turn else (rows, units), dtype),
        compiler_params=pltpu.CompilerParams(vmem_limit_bytes=12 << 20),
        cost_estimate=pl.CostEstimate(
            flops=20 * rows * units, bytes_accessed=cost, transcendentals=rows * units
        ),
    )(pre_act)


def gradient_kernel(thirds, per, *refs):
    pieces, (cot, own, other, first) = refs[thirds:-4], refs[-4:]
    width = first.shape[1]
    for n in range(thirds):

        @pl.when(pl.program_id(0) // per == n)
        def _(n=n):
            first[...] = refs[n][...]

    hidden = jnp.concatenate([first[...], *(ref[...] for ref in pieces)], axis=1)
    half = own.shape[1]
    gradient = jnp.dot(hidden, cot[...], preferred_element_type=f32)
    own[...] = gradient[:, :half]
    other[...] = gradient[:, half:].astype(bf16)


def gradients(thirds, pieces, cot, tile):
    units, rows = pieces[0].shape
    tokens, features = cot.shape
    per = thirds[0].shape[0] // tile
    specs = [
        pl.BlockSpec((tile, rows), lambda j, n=n: (jnp.clip(j - n * per, 0, per - 1), 0))
        for n in range(len(thirds))
    ]
    specs += [pl.BlockSpec((tile, rows), lambda j: (j, 0))] * len(pieces)
    specs += [pl.BlockSpec((tokens, features), lambda j: (0, 0))]
    out = pl.BlockSpec((tile, features // 2), lambda j: (j, 0))
    return pl.pallas_call(
        functools.partial(gradient_kernel, len(thirds), per),
        grid=(units // tile,),
        in_specs=specs,
        out_specs=[out, out],
        out_shape=[
            jax.ShapeDtypeStruct((units, features // 2), f32),
            jax.ShapeDtypeStruct((units, features // 2), bf16),
        ],
        scratch_shapes=[pltpu.VMEM((tile, rows), bf16)],
        compiler_params=pltpu.CompilerParams(vmem_limit_bytes=VMEM),
        cost_estimate=pl.CostEstimate(
            flops=2 * tokens * units * features, bytes_accessed=18 << 20, transcendentals=0
        ),
    )(*thirds, *pieces, cot)


def adam_kernel(own, got, first, second, out):
    out[...] = adam_update(own[...] + got[...].astype(f32), first[...], second[...])


def adam(own, got, first_moment, second_moment, tile):
    units, features = own.shape
    block = pl.BlockSpec((tile, features), lambda j: (j, 0))
    return pl.pallas_call(
        adam_kernel,
        grid=(units // tile,),
        in_specs=[block] * 4,
        out_specs=block,
        out_shape=jax.ShapeDtypeStruct((units, features), bf16),
        compiler_params=pltpu.CompilerParams(vmem_limit_bytes=24 << 20),
        cost_estimate=pl.CostEstimate(
            flops=0, bytes_accessed=12 * units * features, transcendentals=0
        ),
    )(own, got, first_moment, second_moment)


def places(dp, mp):
    block = jnp.arange(16, dtype=jnp.int32)
    z = (mp + block) % 8
    code = ((mp // 8 + block // 8 + dp // 8) % 2) * 4 + (z // 2 - dp // 2) % 4
    slot = sum(jnp.where(code == dx * 4 + dy, i, 0) for i, (dx, dy) in enumerate(ORDER))
    return (slot + 8 * ((z + dp) % 2)).astype(jnp.int32)


def collect_kernel(plan, where, *refs):
    pieces, (own, give) = refs[:-2], refs[-2:]
    depth = pieces[0].shape[1]
    for piece, part, block in plan:
        row = pl.multiple_of(where[block] % 8 * depth, depth)

        @pl.when(where[block] < 8)
        def _():
            own[pl.ds(row, depth)] = pieces[piece][part]

        @pl.when(where[block] >= 8)
        def _():
            give[pl.ds(row, depth)] = pieces[piece][part]


def collect(where, pieces, plan):
    depth, width = pieces[0].shape[1:]
    whole = lambda shape: pl.BlockSpec(shape, lambda j, w: (0,) * len(shape))
    shape = (8 * depth, width)
    return pl.pallas_call(
        functools.partial(collect_kernel, plan),
        out_shape=[jax.ShapeDtypeStruct(shape, bf16)] * 2,
        grid_spec=pltpu.PrefetchScalarGridSpec(
            num_scalar_prefetch=1,
            grid=(1,),
            in_specs=[whole(p.shape) for p in pieces],
            out_specs=[whole(shape)] * 2,
        ),
        compiler_params=pltpu.CompilerParams(vmem_limit_bytes=16 << 20),
        cost_estimate=pl.CostEstimate(
            flops=0, bytes_accessed=60 * depth * width, transcendentals=0
        ),
    )(where, *pieces)


def swap(x):
    return move_dp(x, 0, 0, 1)


def add(*terms):
    return sum(t.astype(f32) for t in terms).astype(bf16)


def add_third(x, i, got):
    size = got.shape[1]
    return add(x, jnp.pad(got, ((0, 0), (i * size, (2 - i) * size))))


def shards(pre_act, cotangent, down_weight, first_moment, second_moment):
    rows, units = pre_act.shape
    features = cotangent.shape[1]
    dp = lax.axis_index("dp")
    mp = lax.axis_index("mp")
    contract_cols = (((1,), (1,)), ((), ()))

    partner = move_mp(cotangent, 1, 0)
    weight = move_dp(down_weight, 0, 0, 1)
    hidden = local(turn_kernel, pre_act, True, bf16, 32 << 20)
    where = places(dp, mp)
    partner, where, _ = barrier((partner, where, hidden))

    both = jnp.stack([cotangent, partner])
    up, down = [both], [both]
    weight = jnp.concatenate([down_weight, weight], axis=1)
    for n in range(3):
        up.append(move_mp(up[-1], 0, 1))
        down.append(move_mp(down[-1], 0, -1))
        if n == 0:
            up[1], down[1], weight = barrier((up[1], down[1], weight))
    x_other = move_dp(hidden, 1, 0, 0)
    y_prev = move_dp(hidden, 0, 1, 0)
    y_next = move_dp(hidden, 0, -1, 0)
    x_other, y_prev = barrier((x_other, y_prev))
    y_far = move_dp(y_next, 0, -1, 0)
    xy_prev = move_dp(x_other, 0, 1, 0)
    xy_next = move_dp(y_next, 1, 0, 0)
    up[3], down[3], y_far, xy_prev, xy_next = barrier(
        (up[3], down[3], y_far, xy_prev, xy_next)
    )
    size = units // 3
    cut = lambda x, i: x[i * size : (i + 1) * size]
    xy_far = [
        move_dp(cut(xy_next, 0), 0, -1, 0),
        move_dp(cut(xy_prev, 1), 0, 1, 0),
        move_dp(cut(y_far, 2), 1, 0, 0),
    ]
    pieces = [both, *down[1:], *up[1:], move_mp(up[3][:1], 0, 1), move_mp(down[3][1:], 0, -1)]
    plan = [(n, f, 8 * f + (n if n < 4 else 11 - n)) for n in range(7) for f in range(2)]
    plan += [(7, 0, 4), (8, 0, 12)]
    cot_own, cot_give = collect(where, barrier(pieces), plan)
    cot_wide = jnp.concatenate([cot_own, swap(cot_give)], axis=1)

    def partial(lo, hi):
        return barrier(
            lax.dot_general(
                cot_wide[lo * rows : hi * rows], weight, contract_cols, preferred_element_type=f32
            ).astype(bf16)
        )

    split = lambda x: [x[k * rows : (k + 1) * rows] for k in range(7)]
    third = lambda x, i: x[:, i * size : (i + 1) * size]
    p_far = partial(0, 1)
    got0 = move_dp(third(p_far, 0), 0, 1, 0)
    got1 = move_dp(third(p_far, 1), 0, -1, 0)
    got2 = move_dp(third(p_far, 2), 1, 0, 0)
    rest = partial(1, 8)
    got0, got1, got2, rest, cot_wide, xy_far = barrier(
        (got0, got1, got2, rest, cot_wide, xy_far)
    )
    p_xy_next, p_xy_prev, p_y_far, p_next, p_prev, p_x, p_mine = split(rest)
    got_x = move_dp(add_third(p_xy_next, 0, got0), 1, 0, 0)
    got_m = move_dp(add_third(p_xy_prev, 1, got1), 0, -1, 0)
    got_y = move_dp(add_third(p_y_far, 2, got2), 0, 1, 0)
    sent = [xy_next, xy_prev, y_far, y_next, y_prev, x_other, hidden]
    grad_own, grad_give = gradients(xy_far, sent, cot_wide, units // 3)
    got_x, got_m, got_y, grad_own, grad_give, p_prev = barrier(
        (got_x, got_m, got_y, grad_own, grad_give, p_prev)
    )
    p_next, p_x, grad_give = barrier((add(p_next, got_x, got_y), add(p_x, got_m), grad_give))
    end_next = move_dp(p_next, 0, 1, 0)
    end_x = move_dp(p_x, 1, 0, 0)
    end_prev = move_dp(p_prev, 0, -1, 0)
    step_update = adam(grad_own, swap(grad_give), first_moment, second_moment, units // 6)
    step_update, pre_act = barrier((step_update, pre_act))
    slopes = local(slope_kernel, pre_act, False, f32, 1)
    end_prev, end_next, end_x, slopes = barrier((end_prev, end_next, end_x, slopes))

    hidden_grad = sum(t.astype(f32) for t in (p_mine, end_prev, end_next, end_x))
    return ((hidden_grad * slopes).astype(bf16), step_update)


def solution(mesh):
    placed = (P("dp", "mp"), P("mp", "dp"), P("mp", "dp"), P("mp", "dp"), P("mp", "dp"))
    return jax.shard_map(
        shards,
        mesh=mesh,
        in_specs=placed,
        out_specs=(P("dp", "mp"), P("mp", "dp")),
        check_vma=False,
    )
```
